32 devices in a mesh: node: 4 (over x, core), rep: 8 (over z, y).
Axes of the slice: x: 2, y: 2, z: 4, core: 2. Of those that a mesh axis runs over, the one named last changes fastest.
Arguments:
- features: bfloat16 [1024, 512], P(('node', 'rep')), may hold values from -6 to 6
- adj_tiles: bfloat16 [8, 4, 6, 128, 128], P('rep', 'node'), may hold values from 0 to 0.024902344
- tile_col: int32 [8, 4, 6], P('rep', 'node'), may hold values from 0 to 1
- tile_count: int32 [8, 4], P('rep', 'node'), may hold values from 1 to 6, as said below
- weight: bfloat16 [512, 512], replicated, may hold values from -0.25 to 0.25
- bias: float32 [512], replicated, may hold values from -3 to 3
- out_grad: bfloat16 [8, 128, 512], P('rep', 'node'), may hold values from -6 to 6
Outputs:
- node_out: bfloat16 [8, 128, 512], P('rep', 'node')
- weight_grad: float32 [512, 512], P('rep')
- input_grad: bfloat16 [1024, 512], P(('node', 'rep'))
The draws below stay inside these ranges and needn't reach their ends.
Inputs may be any that keep to these rules, and one draw needn't show every extreme that they name: `tile_col`: slot k of block row b and part s names a column block of part s; slots at or after tile_count[b, s] are padding and their tiles and columns are not part of A. `tile_count`: the number of live slots of block row b in part s; the most is reached in every draw.
All inputs are finite; a program needn't handle non-finite values.
Results may differ from the reference program's by a relative error of at most 0.014.
Values may be sent and summed in bfloat16 or wider, within the bound.
A program may use at most 64 MiB of HBM per device.

```python
import jax
import jax.numpy as jnp
from jax import lax

H = 512
TILE = 128
SLOT = 6
NODES = 1024
OUT_ROWS = 128
ROW_BLOCKS = 8
PART_BLOCKS = 2
N_NODE = 4
N_REP = 8


def draw_tile_count(key, part):
    key = jax.random.fold_in(key, 7)
    key_heavy, key_light, key_row, key_part = jax.random.split(key, 4)
    heavy = jax.random.randint(key_heavy, (ROW_BLOCKS, N_NODE), 0, 4) == 0
    light = jax.random.randint(key_light, (ROW_BLOCKS, N_NODE), 1, 3)
    counts = jnp.where(heavy, SLOT, light)
    row_pick = jax.random.randint(key_row, (), 0, ROW_BLOCKS)
    part_pick = jax.random.randint(key_part, (), 0, N_NODE)
    counts = counts.at[row_pick, part_pick].set(SLOT)
    return counts.astype(jnp.int32)


def place_ends(entries, stream_key, least, top_value):
    longest = entries.shape.index(max(entries.shape))
    spots = []
    for shift in (0, 1):
        where = [jax.random.randint(jax.random.fold_in(stream_key, axis), (), 0, length) for axis, length in enumerate(entries.shape)]
        where[longest] = (where[longest] + shift) % entries.shape[longest]
        spots.append(tuple(where))
    return entries.at[spots[0]].set(least).at[spots[1]].set(top_value)


def shard_levels(own_key, extent, shards, least, largest):
    gain = 1.0
    for position, parts in shards:
        steps = jax.random.uniform(jax.random.fold_in(jax.random.fold_in(own_key, 6), position), (parts,), jnp.float32, least / len(shards), largest / len(shards))
        gain = gain * jnp.repeat(jnp.exp(steps), extent[position] // parts).reshape((-1,) + (1,) * (len(extent) - 1 - position))
    return gain


def bell_draw(key, extent, spread, reach, cuts=(), kind=jnp.bfloat16):
    entries = jax.random.normal(key, extent, jnp.float32) * spread
    if len(cuts) > 0:
        entries = shard_levels(key, extent, cuts, -0.22, 0.18) * entries
    return jnp.clip(entries, min=-reach, max=reach).astype(kind)


def setup_inputs(seed: int = 0) -> dict:
    arg_keys = jax.random.split(jax.random.key(seed), 8)
    features = bell_draw(arg_keys[0], (NODES, H), 1.0, 6.0, ((0, 32),))
    adj_tiles = jnp.clip(0.024902344 * jax.random.uniform(arg_keys[1], (ROW_BLOCKS, N_NODE, SLOT, TILE, TILE), jnp.float32) ** shard_levels(arg_keys[1], (ROW_BLOCKS, N_NODE, SLOT, TILE, TILE), ((0, 8), (1, 4)), -0.2, 0.2), 0.0, 0.024902344).astype(jnp.bfloat16)
    tile_col = place_ends(jax.random.randint(arg_keys[2], (ROW_BLOCKS, N_NODE, SLOT), 0, PART_BLOCKS), jax.random.fold_in(arg_keys[2], 1), 0, PART_BLOCKS - 1).astype(jnp.int32)
    tile_count = draw_tile_count(jax.random.fold_in(arg_keys[7], 71), 0)
    weight = bell_draw(arg_keys[4], (H, H), H ** -0.5, 0.25)
    bias = bell_draw(arg_keys[5], (H,), 0.5, 3.0, (), jnp.float32)
    out_grad = bell_draw(arg_keys[6], (N_REP, OUT_ROWS, H), 1.0, 6.0, ((0, 8), (1, 4)))
    return dict(features=features, adj_tiles=adj_tiles, tile_col=tile_col, tile_count=tile_count, weight=weight, bias=bias, out_grad=out_grad)


def reference(features, adj_tiles, tile_col, tile_count, weight, bias, out_grad):
    col_blocks = features.reshape(NODES // TILE, TILE, H)
    slot_ids = jnp.arange(SLOT, dtype=jnp.int32)
    part_base = (jnp.arange(N_NODE, dtype=jnp.int32) * PART_BLOCKS)[:, None]

    def forward_row(operands):
        adj_row, cols_row, counts_row = operands
        live_mask = (slot_ids[None, :] < counts_row[:, None]).astype(jnp.float32)
        chosen = col_blocks[(part_base + cols_row).astype(jnp.int32)].astype(jnp.float32)
        masked = adj_row.astype(jnp.float32) * live_mask[:, :, None, None]
        part_sums = jnp.einsum("skij,skjh->sih", masked, chosen).astype(jnp.bfloat16)
        return jnp.sum(part_sums.astype(jnp.float32), axis=0).astype(jnp.bfloat16)

    aggregated = lax.map(forward_row, (adj_tiles, tile_col, tile_count)).reshape(NODES, H)
    preact = jnp.dot(aggregated, weight, preferred_element_type=jnp.float32) + bias
    node_out = jax.nn.silu(preact).astype(jnp.bfloat16).reshape(N_REP, OUT_ROWS, H)
    cotangent = out_grad.reshape(NODES, H).astype(jnp.float32)
    sigma = jax.nn.sigmoid(preact)
    pre_grad = (cotangent * sigma * (1.0 + preact * (1.0 - sigma))).astype(jnp.bfloat16)
    weight_grad = jnp.dot(aggregated.T, pre_grad, preferred_element_type=jnp.float32) * (NODES ** -0.5)
    upstream = jnp.dot(pre_grad, weight.T, preferred_element_type=jnp.float32).astype(jnp.bfloat16)
    up_blocks = upstream.reshape(ROW_BLOCKS, TILE, H)

    def backward_row(grad_total, operands):
        adj_row, cols_row, counts_row, up_row = operands
        live_mask = (slot_ids[None, :] < counts_row[:, None]).astype(jnp.float32)
        masked = adj_row.astype(jnp.float32) * live_mask[:, :, None, None]
        terms = jnp.einsum("skij,ih->skjh", masked, up_row.astype(jnp.float32))
        target = (part_base + cols_row).astype(jnp.int32).reshape(-1)
        grad_total = grad_total.at[target].add(terms.reshape(-1, TILE, H))
        return grad_total, None

    start_total = jnp.zeros((NODES // TILE, TILE, H), jnp.float32)
    grad_total, unused = lax.scan(backward_row, start_total, (adj_tiles, tile_col, tile_count, up_blocks))
    input_grad = grad_total.reshape(NODES, H).astype(jnp.bfloat16)
    return node_out, weight_grad, input_grad
```

```python
import functools

import jax
import jax.numpy as jnp
from jax import lax
from jax.experimental import pallas as pl
from jax.experimental.pallas import tpu as pltpu
from jax.sharding import PartitionSpec as P

LANES = 128
F32 = jnp.float32
BF16 = jnp.bfloat16
MESH = pl.DeviceIdType.MESH


def each(start, stop, body):
    if stop - start <= 8:
        for i in range(start, stop):
            body(i)
    else:
        def step(i, carry):
            body(i)
            return carry
        lax.fori_loop(start, stop, step, 0)


def kernel(
    n_node, n_rep, scale,
    cols, counts, feat, adj, weight, bias, out_grad,
    node_out, weight_grad, input_grad,
    feat_all, adj_v, dense, dense_t, w_v, og_v, sums, sums_in, agg_all, pg_all, no_v,
    wg_out, wg_in, wg_fin, wg_v, ig_out, ig_in, ig_v,
    local_sem, f_send, f_recv, s_send, s_recv, a_send, a_recv, p_send, p_recv,
    w_send, w_recv, i_send, i_recv, v_send, v_recv,
):
    s = lax.axis_index("node")
    r = lax.axis_index("rep")
    row_blocks, slots, tile, _ = adj_v.shape
    rows, width = feat.shape
    part_blocks = n_rep * rows // tile
    per_block = tile // rows
    splits = width // LANES
    groups = n_node // splits

    def node_peer(d):
        return lax.rem(s + d, n_node)

    def rep_peer(d):
        return lax.rem(r + d, n_rep)

    def send(axis, peer, src, dst, send_sems, recv_sems, d):
        return pltpu.make_async_remote_copy(
            src_ref=src, dst_ref=dst, send_sem=send_sems.at[d], recv_sem=recv_sems.at[d],
            device_id={axis: peer}, device_id_type=MESH,
        )

    loads = [
        pltpu.make_async_copy(src, dst, local_sem.at[i])
        for i, (src, dst) in enumerate(
            [(feat, feat_all.at[r]), (adj, adj_v), (weight, w_v), (out_grad, og_v)]
        )
    ]
    for load in loads:
        load.start()

    barrier = pltpu.get_barrier_semaphore()
    each(1, n_rep, lambda d: pl.semaphore_signal(barrier, inc=1, device_id={"rep": rep_peer(d)}, device_id_type=MESH))
    each(1, n_node, lambda d: pl.semaphore_signal(barrier, inc=1, device_id={"node": node_peer(d)}, device_id_type=MESH))
    pl.semaphore_wait(barrier, n_rep + n_node - 2)

    def feat_copy(d):
        return send("rep", rep_peer(d), feat, feat_all.at[r], f_send, f_recv, d)
    each(1, n_rep, lambda d: feat_copy(d).start())

    loads[1].wait()
    for b in range(row_blocks):
        def column(c, b=b):
            total = jnp.zeros((tile, tile), F32)
            for k in range(slots):
                live = jnp.logical_and(k < counts[b], cols[b, k] == c)
                total = total + adj_v[b, k].astype(F32) * jnp.where(live, 1.0, 0.0).astype(F32)
            at = pl.ds(pl.multiple_of(c * tile, tile), tile)
            dense[b, :, at] = total.astype(BF16)
            dense_t[b, at, :] = total.T.astype(BF16)
        each(0, part_blocks, column)
    loads[0].wait()
    loads[2].wait()
    loads[3].wait()
    each(1, n_rep, lambda d: feat_copy(d).wait_recv())

    part = feat_all[...].reshape(n_rep * rows, width)
    for b in range(row_blocks):
        value = jnp.dot(dense[b], part, preferred_element_type=F32).astype(BF16)
        sums[b * per_block:(b + 1) * per_block] = value.reshape(per_block, rows, width)

    def sum_copy(d):
        return send("node", node_peer(d), sums.at[node_peer(d)], sums_in.at[s], s_send, s_recv, d)
    each(1, n_node, lambda d: sum_copy(d).start())
    total = sums[s].astype(F32)
    for d in range(1, n_node):
        sum_copy(d).wait_recv()
        total = total + sums_in[lax.rem(s + n_node - d, n_node)].astype(F32)
    agg = total.astype(BF16)
    agg_all[s] = agg

    def agg_copy(d):
        return send("node", node_peer(d), agg_all.at[s], agg_all.at[s], a_send, a_recv, d)
    each(1, n_node, lambda d: agg_copy(d).start())

    preact = jnp.dot(agg, w_v[...], preferred_element_type=F32) + bias[...]
    sigma = lax.logistic(preact)
    pg_all[s] = (og_v[...].astype(F32) * sigma * (1.0 + preact * (1.0 - sigma))).astype(BF16)

    def pg_copy(d):
        return send("node", node_peer(d), pg_all.at[s], pg_all.at[s], p_send, p_recv, d)
    each(1, n_node, lambda d: pg_copy(d).start())
    no_v[...] = (preact * sigma).astype(BF16)
    store_no = pltpu.make_async_copy(no_v, node_out, local_sem.at[4])
    store_no.start()
    each(1, n_node, lambda d: agg_copy(d).wait_recv())
    each(1, n_node, lambda d: pg_copy(d).wait_recv())

    take = pl.ds(lax.div(s, splits) * splits, splits)
    agg_rows = agg_all[take].reshape(splits * rows, width)
    pg_cols = pg_all[take, :, pl.ds(pl.multiple_of(lax.rem(s, splits) * LANES, LANES), LANES)]
    terms = lax.dot_general(
        agg_rows, pg_cols.reshape(splits * rows, LANES), (((0,), (0,)), ((), ())), preferred_element_type=F32
    )
    wg_out[...] = terms.reshape(wg_out.shape).astype(wg_out.dtype)

    def wg_copy(d):
        return send("rep", rep_peer(d), wg_out.at[rep_peer(d)], wg_in.at[r], w_send, w_recv, d)
    each(1, n_rep, lambda d: wg_copy(d).start())

    upstream = lax.dot_general(
        pg_all[...].reshape(n_node * rows, width), w_v[...], (((1,), (1,)), ((), ())), preferred_element_type=F32
    ).astype(BF16)
    grad = jnp.dot(dense_t[0], upstream[:tile], preferred_element_type=F32)
    for b in range(1, row_blocks):
        grad = grad + jnp.dot(dense_t[b], upstream[b * tile:(b + 1) * tile], preferred_element_type=F32)
    ig_out[...] = grad.reshape(ig_out.shape).astype(BF16)

    def ig_copy(d):
        return send("rep", rep_peer(d), ig_out.at[rep_peer(d)], ig_in.at[r], i_send, i_recv, d)
    each(1, n_rep, lambda d: ig_copy(d).start())

    each(1, n_rep, lambda d: wg_copy(d).wait_recv())
    wg_in[r] = wg_out[r]
    total = jnp.sum(wg_in[...].astype(F32), axis=0)
    wg_fin[s] = (total * scale).astype(wg_fin.dtype)

    def fin_copy(d):
        return send("node", node_peer(d), wg_fin.at[s], wg_fin.at[s], v_send, v_recv, d)
    each(1, n_node, lambda d: fin_copy(d).start())

    each(1, n_rep, lambda d: ig_copy(d).wait_recv())
    ig_in[r] = ig_out[r]
    ig_v[...] = jnp.sum(ig_in[...].astype(F32), axis=0).astype(BF16)
    store_ig = pltpu.make_async_copy(ig_v, input_grad, local_sem.at[5])
    store_ig.start()

    each(1, n_node, lambda d: fin_copy(d).wait_recv())
    for c in range(splits):
        total = wg_fin[c].astype(F32)
        for g in range(1, groups):
            total = total + wg_fin[g * splits + c].astype(F32)
        wg_v[:, c * LANES:(c + 1) * LANES] = total
    store_wg = pltpu.make_async_copy(wg_v, weight_grad, local_sem.at[6])
    store_wg.start()

    for copy in (feat_copy, wg_copy, ig_copy):
        each(1, n_rep, lambda d: copy(d).wait_send())
    for copy in (sum_copy, agg_copy, pg_copy, fin_copy):
        each(1, n_node, lambda d: copy(d).wait_send())
    store_no.wait()
    store_ig.wait()
    store_wg.wait()


def on_device(features, adj_tiles, tile_col, tile_count, weight, bias, out_grad):
    n_node = lax.axis_size("node")
    n_rep = lax.axis_size("rep")
    rows, width = features.shape
    row_blocks, _, slots, tile, _ = adj_tiles.shape
    part_rows = n_rep * rows
    group_rows = n_node * rows
    assert group_rows == row_blocks * tile and part_rows % tile == 0 and tile % rows == 0
    assert width % LANES == 0 and n_node % (width // LANES) == 0
    w_rows = width // n_rep
    w_type = BF16 if w_rows % 16 == 0 else F32
    vmem = pl.BlockSpec(memory_space=pltpu.VMEM)
    smem = pl.BlockSpec(memory_space=pltpu.SMEM)
    hbm = pl.BlockSpec(memory_space=pl.ANY)
    dma = pltpu.SemaphoreType.DMA
    node_out, weight_grad, input_grad = pl.pallas_call(
        functools.partial(kernel, n_node, n_rep, float(part_rows * n_node) ** -0.5),
        out_shape=(
            jax.ShapeDtypeStruct((rows, width), BF16),
            jax.ShapeDtypeStruct((w_rows, width), F32),
            jax.ShapeDtypeStruct((rows, width), BF16),
        ),
        in_specs=[smem, smem, hbm, hbm, hbm, vmem, hbm],
        out_specs=(hbm, hbm, hbm),
        scratch_shapes=[
            pltpu.VMEM((n_rep, rows, width), BF16),
            pltpu.VMEM((row_blocks, slots, tile, tile), BF16),
            pltpu.VMEM((row_blocks, tile, part_rows), BF16),
            pltpu.VMEM((row_blocks, part_rows, tile), BF16),
            pltpu.VMEM((width, width), BF16),
            pltpu.VMEM((rows, width), BF16),
            pltpu.VMEM((n_node, rows, width), BF16),
            pltpu.VMEM((n_node, rows, width), BF16),
            pltpu.VMEM((n_node, rows, width), BF16),
            pltpu.VMEM((n_node, rows, width), BF16),
            pltpu.VMEM((rows, width), BF16),
            pltpu.VMEM((n_rep, w_rows, LANES), w_type),
            pltpu.VMEM((n_rep, w_rows, LANES), w_type),
            pltpu.VMEM((n_node, w_rows, LANES), w_type),
            pltpu.VMEM((w_rows, width), F32),
            pltpu.VMEM((n_rep, rows, width), BF16),
            pltpu.VMEM((n_rep, rows, width), BF16),
            pltpu.VMEM((rows, width), BF16),
            dma((7,)),
            dma((n_rep,)), dma((n_rep,)),
            dma((n_node,)), dma((n_node,)),
            dma((n_node,)), dma((n_node,)),
            dma((n_node,)), dma((n_node,)),
            dma((n_rep,)), dma((n_rep,)),
            dma((n_rep,)), dma((n_rep,)),
            dma((n_node,)), dma((n_node,)),
        ],
        compiler_params=pltpu.CompilerParams(
            collective_id=0, has_side_effects=True, vmem_limit_bytes=40 * 1024 * 1024
        ),
    )(
        tile_col[:, 0], tile_count[:, 0], features, adj_tiles[:, 0], weight, bias.reshape(1, width), out_grad[0]
    )
    return node_out[None], weight_grad, input_grad


def solution(mesh):
    return jax.shard_map(
        on_device,
        mesh=mesh,
        in_specs=(
            P(("node", "rep"), None),
            P("rep", "node", None, None, None),
            P("rep", "node", None),
            P("rep", "node"),
            P(),
            P(),
            P("rep", "node", None),
        ),
        out_specs=(P("rep", "node", None), P("rep", None), P(("node", "rep"), None)),
        check_vma=False,
    )
```

```python
import functools

import jax
import jax.numpy as jnp
from jax import lax
from jax.experimental import pallas as pl
from jax.experimental.pallas import tpu as pltpu
from jax.sharding import PartitionSpec as P

LANES = 128
F32 = jnp.float32
BF16 = jnp.bfloat16
MESH = pl.DeviceIdType.MESH
VMEM_GRANT = 63 * 1024 * 1024


def each(start, stop, body):
    if stop - start <= 8:
        for i in range(start, stop):
            body(i)
    else:
        def step(i, carry):
            body(i)
            return carry
        lax.fori_loop(start, stop, step, 0)


def kernel(
    n_node, n_rep, scale,
    cols, counts, feat, adj, weight, bias, out_grad,
    node_out, weight_grad, input_grad,
    feat_all, adj_v, dense, dense_t, w_v, bias_v, og_v, sums, sums_in, halves, agg_all, pg_all, no_v,
    wg_out, wg_in, wg_fin, wg_v, ig_out, ig_in, ig_v,
    local_sem, f_send, f_recv, w_send, w_recv, i_send, i_recv, o_send, o_recv, s_send, s_recv,
    c_send, c_recv, v_send, v_recv,
):
    s = lax.axis_index("node")
    r = lax.axis_index("rep")
    row_blocks, slots, tile, _ = adj_v.shape
    rows, width = feat.shape
    part_blocks = n_rep * rows // tile
    per_block = tile // rows
    splits = width // LANES
    groups = n_node // splits

    def node_peer(d):
        return lax.rem(s + d, n_node)

    node_half = n_node // 2
    core = lax.rem(s, 2)
    core_pair = s + 1 - 2 * core

    def rep_peer(d):
        return lax.rem(r + d, n_rep)

    def same_core(d):
        return lax.rem(s + 2 * d, n_node)

    def send(axis, peer, src, dst, send_sems, recv_sems, d):
        return pltpu.make_async_remote_copy(
            src_ref=src, dst_ref=dst, send_sem=send_sems.at[d], recv_sem=recv_sems.at[d],
            device_id={axis: peer}, device_id_type=MESH,
        )

    loads = [
        pltpu.make_async_copy(src, dst, local_sem.at[i])
        for i, (src, dst) in enumerate(
            [(feat, feat_all.at[r]), (adj, adj_v), (weight, w_v), (out_grad, og_v.at[lax.div(s, 2)]), (bias, bias_v)]
        )
    ]
    for load in loads:
        load.start()

    barrier = pltpu.get_barrier_semaphore()
    each(1, n_rep, lambda d: pl.semaphore_signal(barrier, inc=1, device_id={"rep": rep_peer(d)}, device_id_type=MESH))
    each(1, n_node, lambda d: pl.semaphore_signal(barrier, inc=1, device_id={"node": node_peer(d)}, device_id_type=MESH))
    pl.semaphore_wait(barrier, n_rep + n_node - 2)

    def feat_copy(d):
        return send("rep", rep_peer(d), feat, feat_all.at[r], f_send, f_recv, d)
    each(1, n_rep, lambda d: feat_copy(d).start())

    def og_copy(d):
        return send("node", same_core(d), out_grad, og_v.at[lax.div(s, 2)], o_send, o_recv, d)
    each(1, node_half, lambda d: og_copy(d).start())

    loads[1].wait()
    for b in range(row_blocks):
        def column(c, b=b):
            total = jnp.zeros((tile, tile), F32)
            for k in range(slots):
                live = jnp.logical_and(k < counts[b], cols[b, k] == c)
                total = total + adj_v[b, k].astype(F32) * jnp.where(live, 1.0, 0.0).astype(F32)
            at = pl.ds(pl.multiple_of(c * tile, tile), tile)
            dense[b, :, at] = total.astype(BF16)
            dense_t[b, at, :] = total.T.astype(BF16)
        each(0, part_blocks, column)
    loads[0].wait()
    loads[2].wait()
    loads[3].wait()
    loads[4].wait()
    each(1, n_rep, lambda d: feat_copy(d).wait_recv())

    part = feat_all[...].reshape(n_rep * rows, width)
    for b in range(row_blocks):
        value = jnp.dot(dense[b], part, preferred_element_type=F32).astype(BF16)
        value = value.reshape(per_block // 2, 2, rows, width)
        at = slice(b * per_block // 2, (b + 1) * per_block // 2)
        sums[0, at] = value[:, 0]
        sums[1, at] = value[:, 1]

    sum_copy = send("node", core_pair, sums.at[1 - core], sums_in, c_send, c_recv, 0)
    sum_copy.start()
    sum_copy.wait_recv()
    halves[lax.div(s, 2)] = (sums[core].astype(F32) + sums_in[...].astype(F32)).astype(BF16)

    def half_copy(d):
        at = halves.at[lax.div(s, 2)]
        return send("node", same_core(d), at, at, s_send, s_recv, d)
    each(1, node_half, lambda d: half_copy(d).start())
    each(1, node_half, lambda d: og_copy(d).wait_recv())
    each(1, node_half, lambda d: half_copy(d).wait_recv())
    agg = jnp.sum(halves[...].astype(F32), axis=0).astype(BF16)
    agg_all[core] = agg
    agg_copy = send("node", core_pair, agg_all.at[core], agg_all.at[core], c_send, c_recv, 1)
    agg_copy.start()

    preact = jnp.dot(agg.reshape(node_half * rows, width), w_v[...], preferred_element_type=F32) + bias_v[...]
    sigma = lax.logistic(preact)
    cotangent = og_v[...].reshape(node_half * rows, width).astype(F32)
    pre_grad = (cotangent * sigma * (1.0 + preact * (1.0 - sigma))).astype(BF16)
    pg_all[core] = pre_grad.reshape(node_half, rows, width)
    pg_copy = send("node", core_pair, pg_all.at[core], pg_all.at[core], c_send, c_recv, 2)
    pg_copy.start()
    no_v[...] = (preact * sigma).astype(BF16).reshape(node_half, rows, width)
    store_no = pltpu.make_async_copy(no_v.at[lax.div(s, 2)], node_out, local_sem.at[6])
    store_no.start()
    agg_copy.wait_recv()
    pg_copy.wait_recv()

    share = splits // 2
    take = pl.ds(lax.div(s, splits) * share, share)
    agg_rows = agg_all[:, take].reshape(splits * rows, width)
    pg_cols = pg_all[:, take, :, pl.ds(pl.multiple_of(lax.rem(s, splits) * LANES, LANES), LANES)]
    terms = lax.dot_general(
        agg_rows, pg_cols.reshape(splits * rows, LANES), (((0,), (0,)), ((), ())), preferred_element_type=F32
    )
    wg_out[...] = terms.reshape(wg_out.shape).astype(wg_out.dtype)

    def wg_copy(d):
        return send("rep", rep_peer(d), wg_out.at[rep_peer(d)], wg_in.at[r], w_send, w_recv, d)
    each(1, n_rep, lambda d: wg_copy(d).start())

    up = lax.dot_general(
        pg_all[...].reshape(n_node * rows, width), w_v[...], (((1,), (1,)), ((), ())), preferred_element_type=F32
    ).astype(BF16).reshape(2, node_half, rows, width)
    upstream = jnp.stack([up[i % 2, i // 2] for i in range(n_node)]).reshape(n_node * rows, width)
    grad = jnp.dot(dense_t[0], upstream[:tile], preferred_element_type=F32)
    for b in range(1, row_blocks):
        grad = grad + jnp.dot(dense_t[b], upstream[b * tile:(b + 1) * tile], preferred_element_type=F32)
    ig_out[...] = grad.reshape(ig_out.shape).astype(BF16)

    def ig_copy(d):
        return send("rep", rep_peer(d), ig_out.at[rep_peer(d)], ig_in.at[r], i_send, i_recv, d)
    each(1, n_rep, lambda d: ig_copy(d).start())

    each(1, n_rep, lambda d: wg_copy(d).wait_recv())
    wg_in[r] = wg_out[r]
    wg_fin[s] = (jnp.sum(wg_in[...].astype(F32), axis=0) * scale).astype(wg_fin.dtype)

    def fin_copy(d):
        return send("node", node_peer(d), wg_fin.at[s], wg_fin.at[s], v_send, v_recv, d)
    each(1, n_node, lambda d: fin_copy(d).start())

    each(1, n_rep, lambda d: ig_copy(d).wait_recv())
    ig_in[r] = ig_out[r]
    ig_v[...] = jnp.sum(ig_in[...].astype(F32), axis=0).astype(BF16)
    store_ig = pltpu.make_async_copy(ig_v, input_grad, local_sem.at[5])
    store_ig.start()

    each(1, n_node, lambda d: fin_copy(d).wait_recv())
    for c in range(splits):
        total = wg_fin[c].astype(F32)
        for g in range(1, groups):
            total = total + wg_fin[g * splits + c].astype(F32)
        wg_v[:, c * LANES:(c + 1) * LANES] = total
    store_wg = pltpu.make_async_copy(wg_v, weight_grad, local_sem.at[7])
    store_wg.start()

    for copy in (sum_copy, agg_copy, pg_copy):
        copy.wait_send()
    for copy in (feat_copy, wg_copy, ig_copy):
        each(1, n_rep, lambda d: copy(d).wait_send())
    for copy in (og_copy, half_copy):
        each(1, node_half, lambda d: copy(d).wait_send())
    each(1, n_node, lambda d: fin_copy(d).wait_send())
    store_no.wait()
    store_ig.wait()
    store_wg.wait()


def store_kernel(a, b, c, a_out, b_out, c_out, a_v, b_v, c_v, sems):
    moves = [(b, b_v, b_out), (a, a_v, a_out), (c, c_v, c_out)]
    loads = [pltpu.make_async_copy(src, mid, sems.at[i]) for i, (src, mid, _) in enumerate(moves)]
    stores = [pltpu.make_async_copy(mid, dst, sems.at[i + 3]) for i, (_, mid, dst) in enumerate(moves)]
    for load in loads:
        load.start()
    for load, copy in zip(loads, stores):
        load.wait()
        copy.start()
    for copy in stores:
        copy.wait()


def store(*arrays):
    hbm = pl.BlockSpec(memory_space=pl.ANY)
    return pl.pallas_call(
        store_kernel,
        out_shape=tuple(jax.ShapeDtypeStruct(a.shape, a.dtype) for a in arrays),
        in_specs=[hbm] * 3,
        out_specs=(hbm,) * 3,
        scratch_shapes=[*[pltpu.VMEM(a.shape, a.dtype) for a in arrays], pltpu.SemaphoreType.DMA((6,))],
        compiler_params=pltpu.CompilerParams(vmem_limit_bytes=VMEM_GRANT),
    )(*arrays)


def on_device(features, adj_tiles, tile_col, tile_count, weight, bias, out_grad):
    n_node = lax.axis_size("node")
    n_rep = lax.axis_size("rep")
    rows, width = features.shape
    row_blocks, _, slots, tile, _ = adj_tiles.shape
    part_rows = n_rep * rows
    group_rows = n_node * rows
    assert group_rows == row_blocks * tile and part_rows % tile == 0 and tile % rows == 0
    assert width % LANES == 0 and n_node % (width // LANES) == 0
    assert n_node % 2 == 0 and tile // rows % 2 == 0 and width // LANES % 2 == 0
    node_half = n_node // 2
    w_rows = width // n_rep
    w_type = BF16 if w_rows % 16 == 0 else F32
    smem = pl.BlockSpec(memory_space=pltpu.SMEM)
    hbm = pl.BlockSpec(memory_space=pl.ANY)
    dma = pltpu.SemaphoreType.DMA
    node_out, weight_grad, input_grad = pl.pallas_call(
        functools.partial(kernel, n_node, n_rep, float(part_rows * n_node) ** -0.5),
        out_shape=(
            jax.ShapeDtypeStruct((rows, width), BF16),
            jax.ShapeDtypeStruct((w_rows, width), F32),
            jax.ShapeDtypeStruct((rows, width), BF16),
        ),
        in_specs=[smem, smem] + [hbm] * 5,
        out_specs=(hbm, hbm, hbm),
        scratch_shapes=[
            pltpu.VMEM((n_rep, rows, width), BF16),
            pltpu.VMEM((row_blocks, slots, tile, tile), BF16),
            pltpu.VMEM((row_blocks, tile, part_rows), BF16),
            pltpu.VMEM((row_blocks, part_rows, tile), BF16),
            pltpu.VMEM((width, width), BF16),
            pltpu.VMEM((1, width), F32),
            pltpu.VMEM((node_half, rows, width), BF16),
            pltpu.VMEM((2, node_half, rows, width), BF16),
            pltpu.VMEM((node_half, rows, width), BF16),
            pltpu.VMEM((node_half, node_half, rows, width), BF16),
            pltpu.VMEM((2, node_half, rows, width), BF16),
            pltpu.VMEM((2, node_half, rows, width), BF16),
            pltpu.VMEM((node_half, rows, width), BF16),
            pltpu.VMEM((n_rep, w_rows, LANES), w_type),
            pltpu.VMEM((n_rep, w_rows, LANES), w_type),
            pltpu.VMEM((n_node, w_rows, LANES), w_type),
            pltpu.VMEM((w_rows, width), F32),
            pltpu.VMEM((n_rep, rows, width), BF16),
            pltpu.VMEM((n_rep, rows, width), BF16),
            pltpu.VMEM((rows, width), BF16),
            dma((8,)),
            *[dma((n_rep,))] * 6,
            *[dma((node_half,))] * 4,
            *[dma((3,))] * 2,
            *[dma((n_node,))] * 2,
        ],
        compiler_params=pltpu.CompilerParams(
            collective_id=0, has_side_effects=True, vmem_limit_bytes=VMEM_GRANT
        ),
    )(
        tile_col[:, 0], tile_count[:, 0], features, adj_tiles[:, 0], weight, bias.reshape(1, width), out_grad[0]
    )
    node_out, weight_grad, input_grad = store(node_out, weight_grad, input_grad)
    return node_out[None], weight_grad, input_grad


def solution(mesh):
    return jax.shard_map(
        on_device,
        mesh=mesh,
        in_specs=(
            P(("node", "rep"), None),
            P("rep", "node", None, None, None),
            P("rep", "node", None),
            P("rep", "node"),
            P(),
            P(),
            P("rep", "node", None),
        ),
        out_specs=(P("rep", "node", None), P("rep", None), P(("node", "rep"), None)),
        check_vma=False,
    )
```

```python
import functools

import jax
import jax.numpy as jnp
from jax import lax
from jax.experimental import pallas as pl
from jax.experimental.pallas import tpu as pltpu
from jax.sharding import PartitionSpec as P

LANES = 128
F32 = jnp.float32
BF16 = jnp.bfloat16
MESH = pl.DeviceIdType.MESH
VMEM_GRANT = 40 * 1024 * 1024


def each(start, stop, body):
    if stop - start <= 8:
        for i in range(start, stop):
            body(i)
    else:
        def step(i, carry):
            body(i)
            return carry
        lax.fori_loop(start, stop, step, 0)


def kernel(
    n_node, n_rep, scale,
    counts, cols_in, feat, adj, weight, bias, out_grad,
    node_out, weight_grad, input_grad,
    cols, feat_all, adj_v, dense, dense_t, w_v, bias_v, og_v, sums, sums_in, halves, agg_all, agg_t, pg_all, no_v,
    wg_out, wg_in, wg_fin, wg_v, ig_out, ig_in, ig_v,
    local_sem, f_send, f_recv, w_send, w_recv, i_send, i_recv, o_send, o_recv, s_send, s_recv,
    c_send, c_recv, v_send, v_recv,
):
    s = lax.axis_index("node")
    r = lax.axis_index("rep")
    row_blocks, slots, tile, _ = adj_v.shape
    rows, width = feat.shape
    part_blocks = n_rep * rows // tile
    per_block = tile // rows
    splits = width // LANES
    groups = n_node // splits

    def node_peer(d):
        return lax.rem(s + d, n_node)

    node_half = n_node // 2
    core = lax.rem(s, 2)
    core_pair = s + 1 - 2 * core

    def rep_peer(d):
        return lax.rem(r + d, n_rep)

    def same_core(d):
        return lax.rem(s + 2 * d, n_node)

    def send(axis, peer, src, dst, send_sems, recv_sems, d):
        return pltpu.make_async_remote_copy(
            src_ref=src, dst_ref=dst, send_sem=send_sems.at[d], recv_sem=recv_sems.at[d],
            device_id={axis: peer}, device_id_type=MESH,
        )

    loads = [
        pltpu.make_async_copy(src, dst, local_sem.at[i])
        for i, (src, dst) in enumerate(
            [(feat, feat_all.at[r]), (adj, adj_v), (weight, w_v), (out_grad, og_v.at[lax.div(s, 2)]), (bias, bias_v), (cols_in, cols)]
        )
    ]
    for load in loads:
        load.start()

    barrier = pltpu.get_barrier_semaphore()
    each(1, n_rep, lambda d: pl.semaphore_signal(barrier, inc=1, device_id={"rep": rep_peer(d)}, device_id_type=MESH))
    each(1, n_node, lambda d: pl.semaphore_signal(barrier, inc=1, device_id={"node": node_peer(d)}, device_id_type=MESH))
    pl.semaphore_wait(barrier, n_rep + n_node - 2)

    def feat_copy(d):
        return send("rep", rep_peer(d), feat, feat_all.at[r], f_send, f_recv, d)
    each(1, n_rep, lambda d: feat_copy(d).start())

    def og_copy(d):
        return send("node", same_core(d), out_grad, og_v.at[lax.div(s, 2)], o_send, o_recv, d)
    each(1, node_half, lambda d: og_copy(d).start())

    loads[1].wait()
    loads[5].wait()
    for b in range(row_blocks):
        def column(c, b=b):
            total = jnp.zeros((tile, tile), F32)
            for k in range(slots):
                live = jnp.logical_and(k < counts[b], cols[b, k] == c)
                total = total + adj_v[b, k].astype(F32) * jnp.where(live, 1.0, 0.0).astype(F32)
            at = pl.ds(pl.multiple_of(c * tile, tile), tile)
            dense[b, :, at] = total.astype(BF16)
            dense_t[b, at, :] = total.T.astype(BF16)
        each(0, part_blocks, column)
    loads[0].wait()
    loads[2].wait()
    loads[3].wait()
    loads[4].wait()
    each(1, n_rep, lambda d: feat_copy(d).wait_recv())

    part = feat_all[...].reshape(n_rep * rows, width)
    for b in range(row_blocks):
        value = jnp.dot(dense[b], part, preferred_element_type=F32).astype(BF16)
        value = value.reshape(per_block // 2, 2, rows, width)
        at = slice(b * per_block // 2, (b + 1) * per_block // 2)
        sums[0, at] = value[:, 0]
        sums[1, at] = value[:, 1]

    sum_copy = send("node", core_pair, sums.at[1 - core], sums_in, c_send, c_recv, 0)
    sum_copy.start()
    sum_copy.wait_recv()
    halves[lax.div(s, 2)] = (sums[core].astype(F32) + sums_in[...].astype(F32)).astype(BF16)

    def half_copy(d):
        at = halves.at[lax.div(s, 2)]
        return send("node", same_core(d), at, at, s_send, s_recv, d)
    each(1, node_half, lambda d: half_copy(d).start())
    each(1, node_half, lambda d: og_copy(d).wait_recv())
    each(1, node_half, lambda d: half_copy(d).wait_recv())
    agg = jnp.sum(halves[...].astype(F32), axis=0).astype(BF16)
    agg_all[core] = agg
    agg_copy = send("node", core_pair, agg_all.at[core], agg_all.at[core], c_send, c_recv, 1)
    agg_copy.start()

    preact = jnp.dot(agg.reshape(node_half * rows, width), w_v[...], preferred_element_type=F32) + bias_v[...]
    sigma = lax.logistic(preact)
    cotangent = og_v[...].reshape(node_half * rows, width).astype(F32)
    pre_grad = (cotangent * sigma * (1.0 + preact * (1.0 - sigma))).astype(BF16)
    pg_all[core] = pre_grad.reshape(node_half, rows, width)
    pg_copy = send("node", core_pair, pg_all.at[core], pg_all.at[core], c_send, c_recv, 2)
    pg_copy.start()
    no_v[...] = (preact * sigma).astype(BF16).reshape(node_half, rows, width)
    store_no = pltpu.make_async_copy(no_v.at[lax.div(s, 2)], node_out, local_sem.at[8])
    store_no.start()
    share = splits // 2
    take = pl.ds(lax.div(s, splits) * share, share)
    agg_copy.wait_recv()
    agg_t[...] = agg_all[:, take].reshape(splits * rows, width).T
    pg_copy.wait_recv()

    pg_cols = pg_all[:, take, :, pl.ds(pl.multiple_of(lax.rem(s, splits) * LANES, LANES), LANES)]
    terms = jnp.dot(agg_t[...], pg_cols.reshape(splits * rows, LANES), preferred_element_type=F32)
    wg_out[...] = terms.reshape(wg_out.shape).astype(wg_out.dtype)

    def wg_copy(d):
        return send("rep", rep_peer(d), wg_out.at[rep_peer(d)], wg_in.at[r], w_send, w_recv, d)
    each(1, n_rep, lambda d: wg_copy(d).start())

    up = lax.dot_general(
        pg_all[...].reshape(n_node * rows, width), w_v[...], (((1,), (1,)), ((), ())), preferred_element_type=F32
    ).astype(BF16).reshape(2, node_half, rows, width)
    upstream = jnp.stack([up[i % 2, i // 2] for i in range(n_node)]).reshape(n_node * rows, width)
    grad = jnp.dot(dense_t[0], upstream[:tile], preferred_element_type=F32)
    for b in range(1, row_blocks):
        grad = grad + jnp.dot(dense_t[b], upstream[b * tile:(b + 1) * tile], preferred_element_type=F32)
    ig_out[...] = grad.reshape(ig_out.shape).astype(BF16)

    def ig_copy(d):
        return send("rep", rep_peer(d), ig_out.at[rep_peer(d)], ig_in.at[r], i_send, i_recv, d)
    each(1, n_rep, lambda d: ig_copy(d).start())

    each(1, n_rep, lambda d: wg_copy(d).wait_recv())
    wg_in[r] = wg_out[r]
    wg_fin[s] = (jnp.sum(wg_in[...].astype(F32), axis=0) * scale).astype(wg_fin.dtype)

    def fin_copy(d):
        return send("node", node_peer(d), wg_fin.at[s], wg_fin.at[s], v_send, v_recv, d)
    each(1, n_node, lambda d: fin_copy(d).start())

    each(1, n_rep, lambda d: ig_copy(d).wait_recv())
    ig_in[r] = ig_out[r]
    ig_v[...] = jnp.sum(ig_in[...].astype(F32), axis=0).astype(BF16)
    store_ig = pltpu.make_async_copy(ig_v, input_grad, local_sem.at[7])
    store_ig.start()

    each(1, n_node, lambda d: fin_copy(d).wait_recv())
    for c in range(splits):
        total = wg_fin[c].astype(F32)
        for g in range(1, groups):
            total = total + wg_fin[g * splits + c].astype(F32)
        wg_v[:, c * LANES:(c + 1) * LANES] = total
    store_wg = pltpu.make_async_copy(wg_v, weight_grad, local_sem.at[9])
    store_wg.start()

    for copy in (sum_copy, agg_copy, pg_copy):
        copy.wait_send()
    for copy in (feat_copy, wg_copy, ig_copy):
        each(1, n_rep, lambda d: copy(d).wait_send())
    for copy in (og_copy, half_copy):
        each(1, node_half, lambda d: copy(d).wait_send())
    each(1, n_node, lambda d: fin_copy(d).wait_send())
    store_no.wait()
    store_ig.wait()
    store_wg.wait()


def store_kernel(a, b, c, a_out, b_out, c_out, sems):
    copies = [
        pltpu.make_async_copy(src, dst, sems.at[i]) for i, (src, dst) in enumerate([(b, b_out), (a, a_out), (c, c_out)])
    ]
    for copy in copies:
        copy.start()
    for copy in copies:
        copy.wait()


def store(*arrays):
    hbm = pl.BlockSpec(memory_space=pl.ANY)
    return pl.pallas_call(
        store_kernel,
        out_shape=tuple(jax.ShapeDtypeStruct(a.shape, a.dtype) for a in arrays),
        in_specs=[hbm] * 3,
        out_specs=(hbm,) * 3,
        scratch_shapes=[pltpu.SemaphoreType.DMA((3,))],
        compiler_params=pltpu.CompilerParams(vmem_limit_bytes=1024 * 1024),
    )(*arrays)


def on_device(features, adj_tiles, tile_col, tile_count, weight, bias, out_grad):
    n_node = lax.axis_size("node")
    n_rep = lax.axis_size("rep")
    rows, width = features.shape
    row_blocks, _, slots, tile, _ = adj_tiles.shape
    part_rows = n_rep * rows
    group_rows = n_node * rows
    assert group_rows == row_blocks * tile and part_rows % tile == 0 and tile % rows == 0
    assert width % LANES == 0 and n_node % (width // LANES) == 0
    assert n_node % 2 == 0 and tile // rows % 2 == 0 and width // LANES % 2 == 0
    node_half = n_node // 2
    w_rows = width // n_rep
    w_type = BF16 if w_rows % 16 == 0 else F32
    hbm = pl.BlockSpec(memory_space=pl.ANY)
    dma = pltpu.SemaphoreType.DMA
    node_out, weight_grad, input_grad = pl.pallas_call(
        functools.partial(kernel, n_node, n_rep, float(part_rows * n_node) ** -0.5),
        out_shape=(
            jax.ShapeDtypeStruct((rows, width), BF16),
            jax.ShapeDtypeStruct((w_rows, width), F32),
            jax.ShapeDtypeStruct((rows, width), BF16),
        ),
        in_specs=[pl.BlockSpec(memory_space=pltpu.SMEM)] + [hbm] * 6,
        out_specs=(hbm, hbm, hbm),
        scratch_shapes=[
            pltpu.SMEM((row_blocks, slots), jnp.int32),
            pltpu.VMEM((n_rep, rows, width), BF16),
            pltpu.VMEM((row_blocks, slots, tile, tile), BF16),
            pltpu.VMEM((row_blocks, tile, part_rows), BF16),
            pltpu.VMEM((row_blocks, part_rows, tile), BF16),
            pltpu.VMEM((width, width), BF16),
            pltpu.VMEM((1, width), F32),
            pltpu.VMEM((node_half, rows, width), BF16),
            pltpu.VMEM((2, node_half, rows, width), BF16),
            pltpu.VMEM((node_half, rows, width), BF16),
            pltpu.VMEM((node_half, node_half, rows, width), BF16),
            pltpu.VMEM((2, node_half, rows, width), BF16),
            pltpu.VMEM((width, width // LANES * rows), BF16),
            pltpu.VMEM((2, node_half, rows, width), BF16),
            pltpu.VMEM((node_half, rows, width), BF16),
            pltpu.VMEM((n_rep, w_rows, LANES), w_type),
            pltpu.VMEM((n_rep, w_rows, LANES), w_type),
            pltpu.VMEM((n_node, w_rows, LANES), w_type),
            pltpu.VMEM((w_rows, width), F32),
            pltpu.VMEM((n_rep, rows, width), BF16),
            pltpu.VMEM((n_rep, rows, width), BF16),
            pltpu.VMEM((rows, width), BF16),
            dma((10,)),
            *[dma((n_rep,))] * 6,
            *[dma((node_half,))] * 4,
            *[dma((3,))] * 2,
            *[dma((n_node,))] * 2,
        ],
        compiler_params=pltpu.CompilerParams(
            collective_id=0, has_side_effects=True, vmem_limit_bytes=VMEM_GRANT
        ),
    )(
        tile_count[:, 0],
        *[
            pltpu.with_memory_space_constraint(x, pltpu.HBM)
            for x in (tile_col[:, 0], features, adj_tiles[:, 0], weight, bias.reshape(1, width), out_grad[0])
        ],
    )
    node_out, weight_grad, input_grad = store(node_out, weight_grad, input_grad)
    return node_out[None], weight_grad, input_grad


def solution(mesh):
    return jax.shard_map(
        on_device,
        mesh=mesh,
        in_specs=(
            P(("node", "rep"), None),
            P("rep", "node", None, None, None),
            P("rep", "node", None),
            P("rep", "node"),
            P(),
            P(),
            P("rep", "node", None),
        ),
        out_specs=(P("rep", "node", None), P("rep", None), P(("node", "rep"), None)),
        check_vma=False,
    )
```

```python
import functools

import jax
import jax.numpy as jnp
from jax import lax
from jax.experimental import pallas as pl
from jax.experimental.pallas import tpu as pltpu
from jax.sharding import PartitionSpec as P

LANES = 128
F32 = jnp.float32
BF16 = jnp.bfloat16
MESH = pl.DeviceIdType.MESH
VMEM_GRANT = 40 * 1024 * 1024


def each(start, stop, body):
    if stop - start <= 8:
        for i in range(start, stop):
            body(i)
    else:
        def step(i, carry):
            body(i)
            return carry
        lax.fori_loop(start, stop, step, 0)


def kernel(
    n_node, n_rep, scale,
    counts, cols_in, feat, adj, weight, bias, out_grad,
    node_out, weight_grad, input_grad,
    cols, feat_all, adj_v, dense, dense_t, w_v, bias_v, og_v, sums, sums_in, halves, agg_all, agg_t, pg_all, no_v,
    wg_out, wg_in, wg_fin, wg_v, ig_out, ig_in, ig_v,
    local_sem, f_send, f_recv, w_send, w_recv, i_send, i_recv, o_send, o_recv, s_send, s_recv,
    c_send, c_recv, v_send, v_recv,
):
    s = lax.axis_index("node")
    r = lax.axis_index("rep")
    row_blocks, slots, tile, _ = adj_v.shape
    rows, width = feat.shape
    part_blocks = n_rep * rows // tile
    per_block = tile // rows
    splits = width // LANES
    groups = n_node // splits

    def node_peer(d):
        return lax.rem(s + d, n_node)

    node_half = n_node // 2
    core = lax.rem(s, 2)
    core_pair = s + 1 - 2 * core

    def rep_peer(d):
        return lax.rem(r + d, n_rep)

    def same_core(d):
        return lax.rem(s + 2 * d, n_node)

    def send(axis, peer, src, dst, send_sems, recv_sems, d):
        return pltpu.make_async_remote_copy(
            src_ref=src, dst_ref=dst, send_sem=send_sems.at[d], recv_sem=recv_sems.at[d],
            device_id={axis: peer}, device_id_type=MESH,
        )

    barrier = pltpu.get_barrier_semaphore()
    each(1, n_rep, lambda d: pl.semaphore_signal(barrier, inc=1, device_id={"rep": rep_peer(d)}, device_id_type=MESH))
    each(1, n_node, lambda d: pl.semaphore_signal(barrier, inc=1, device_id={"node": node_peer(d)}, device_id_type=MESH))
    loads = [
        pltpu.make_async_copy(src, dst, local_sem.at[i])
        for i, (src, dst) in enumerate(
            [(feat, feat_all.at[r]), (adj, adj_v), (weight, w_v), (out_grad, og_v.at[lax.div(s, 2)]), (bias, bias_v), (cols_in, cols)]
        )
    ]
    for load in loads:
        load.start()
    loads[0].wait()
    pl.semaphore_wait(barrier, n_rep + n_node - 2)

    def feat_copy(d):
        return send("rep", rep_peer(d), feat_all.at[r], feat_all.at[r], f_send, f_recv, d)
    each(1, n_rep, lambda d: feat_copy(d).start())

    def og_copy(d):
        return send("node", same_core(d), out_grad, og_v.at[lax.div(s, 2)], o_send, o_recv, d)
    each(1, node_half, lambda d: og_copy(d).start())

    loads[1].wait()
    loads[5].wait()
    for b in range(row_blocks):
        def column(c, b=b):
            total = jnp.zeros((tile, tile), F32)
            for k in range(slots):
                live = jnp.logical_and(k < counts[b], cols[b, k] == c)
                total = total + adj_v[b, k].astype(F32) * jnp.where(live, 1.0, 0.0).astype(F32)
            at = pl.ds(pl.multiple_of(c * tile, tile), tile)
            dense[b, :, at] = total.astype(BF16)
            dense_t[b, at, :] = total.T.astype(BF16)
        each(0, part_blocks, column)
    loads[2].wait()
    loads[3].wait()
    loads[4].wait()
    each(1, n_rep, lambda d: feat_copy(d).wait_recv())

    part = feat_all[...].reshape(n_rep * rows, width)
    for b in range(row_blocks):
        value = jnp.dot(dense[b], part, preferred_element_type=F32).astype(BF16)
        value = value.reshape(per_block // 2, 2, rows, width)
        at = slice(b * per_block // 2, (b + 1) * per_block // 2)
        sums[0, at] = value[:, 0]
        sums[1, at] = value[:, 1]

    sum_copy = send("node", core_pair, sums.at[1 - core], sums_in, c_send, c_recv, 0)
    sum_copy.start()
    sum_copy.wait_recv()
    halves[lax.div(s, 2)] = (sums[core].astype(F32) + sums_in[...].astype(F32)).astype(BF16)

    def half_copy(d):
        at = halves.at[lax.div(s, 2)]
        return send("node", same_core(d), at, at, s_send, s_recv, d)
    each(1, node_half, lambda d: half_copy(d).start())
    each(1, node_half, lambda d: og_copy(d).wait_recv())
    each(1, node_half, lambda d: half_copy(d).wait_recv())
    agg = jnp.sum(halves[...].astype(F32), axis=0).astype(BF16)
    agg_all[core] = agg
    agg_copy = send("node", core_pair, agg_all.at[core], agg_all.at[core], c_send, c_recv, 1)
    agg_copy.start()

    preact = jnp.dot(agg.reshape(node_half * rows, width), w_v[...], preferred_element_type=F32) + bias_v[...]
    sigma = lax.logistic(preact)
    cotangent = og_v[...].reshape(node_half * rows, width).astype(F32)
    pre_grad = (cotangent * sigma * (1.0 + preact * (1.0 - sigma))).astype(BF16)
    pg_all[core] = pre_grad.reshape(node_half, rows, width)
    pg_copy = send("node", core_pair, pg_all.at[core], pg_all.at[core], c_send, c_recv, 2)
    pg_copy.start()
    no_v[...] = (preact * sigma).astype(BF16).reshape(node_half, rows, width)
    store_no = pltpu.make_async_copy(no_v.at[lax.div(s, 2)], node_out, local_sem.at[8])
    store_no.start()
    share = splits // 2
    take = pl.ds(lax.div(s, splits) * share, share)
    agg_copy.wait_recv()
    agg_t[...] = agg_all[:, take].reshape(splits * rows, width).T
    pg_copy.wait_recv()

    pg_cols = pg_all[:, take, :, pl.ds(pl.multiple_of(lax.rem(s, splits) * LANES, LANES), LANES)]
    terms = jnp.dot(agg_t[...], pg_cols.reshape(splits * rows, LANES), preferred_element_type=F32)
    wg_out[...] = terms.reshape(wg_out.shape).astype(wg_out.dtype)

    def wg_copy(d):
        return send("rep", rep_peer(d), wg_out.at[rep_peer(d)], wg_in.at[r], w_send, w_recv, d)
    each(1, n_rep, lambda d: wg_copy(d).start())

    up = lax.dot_general(
        pg_all[...].reshape(n_node * rows, width), w_v[...], (((1,), (1,)), ((), ())), preferred_element_type=F32
    ).astype(BF16).reshape(2, node_half, rows, width)
    upstream = jnp.stack([up[i % 2, i // 2] for i in range(n_node)]).reshape(n_node * rows, width)
    grad = jnp.dot(dense_t[0], upstream[:tile], preferred_element_type=F32)
    for b in range(1, row_blocks):
        grad = grad + jnp.dot(dense_t[b], upstream[b * tile:(b + 1) * tile], preferred_element_type=F32)
    ig_out[...] = grad.reshape(ig_out.shape).astype(BF16)

    def ig_copy(d):
        return send("rep", rep_peer(d), ig_out.at[rep_peer(d)], ig_in.at[r], i_send, i_recv, d)
    each(1, n_rep, lambda d: ig_copy(d).start())

    each(1, n_rep, lambda d: wg_copy(d).wait_recv())
    wg_in[r] = wg_out[r]
    wg_fin[s] = (jnp.sum(wg_in[...].astype(F32), axis=0) * scale).astype(wg_fin.dtype)

    def fin_copy(d):
        return send("node", node_peer(d), wg_fin.at[s], wg_fin.at[s], v_send, v_recv, d)
    each(1, n_node, lambda d: fin_copy(d).start())

    each(1, n_rep, lambda d: ig_copy(d).wait_recv())
    ig_in[r] = ig_out[r]
    ig_v[...] = jnp.sum(ig_in[...].astype(F32), axis=0).astype(BF16)
    store_ig = pltpu.make_async_copy(ig_v, input_grad, local_sem.at[7])
    store_ig.start()

    each(1, n_node, lambda d: fin_copy(d).wait_recv())
    for c in range(splits):
        total = wg_fin[c].astype(F32)
        for g in range(1, groups):
            total = total + wg_fin[g * splits + c].astype(F32)
        wg_v[:, c * LANES:(c + 1) * LANES] = total
    store_wg = pltpu.make_async_copy(wg_v, weight_grad, local_sem.at[9])
    store_wg.start()

    for copy in (sum_copy, agg_copy, pg_copy):
        copy.wait_send()
    for copy in (feat_copy, wg_copy, ig_copy):
        each(1, n_rep, lambda d: copy(d).wait_send())
    for copy in (og_copy, half_copy):
        each(1, node_half, lambda d: copy(d).wait_send())
    each(1, n_node, lambda d: fin_copy(d).wait_send())
    store_no.wait()
    store_ig.wait()
    store_wg.wait()


def store_kernel(a, b, c, a_out, b_out, c_out, sems):
    copies = [
        pltpu.make_async_copy(src, dst, sems.at[i]) for i, (src, dst) in enumerate([(b, b_out), (a, a_out), (c, c_out)])
    ]
    for copy in copies:
        copy.start()
    for copy in copies:
        copy.wait()


def store(*arrays):
    hbm = pl.BlockSpec(memory_space=pl.ANY)
    return pl.pallas_call(
        store_kernel,
        out_shape=tuple(jax.ShapeDtypeStruct(a.shape, a.dtype) for a in arrays),
        in_specs=[hbm] * 3,
        out_specs=(hbm,) * 3,
        scratch_shapes=[pltpu.SemaphoreType.DMA((3,))],
        compiler_params=pltpu.CompilerParams(vmem_limit_bytes=1024 * 1024),
    )(*arrays)


def on_device(features, adj_tiles, tile_col, tile_count, weight, bias, out_grad):
    n_node = lax.axis_size("node")
    n_rep = lax.axis_size("rep")
    rows, width = features.shape
    row_blocks, _, slots, tile, _ = adj_tiles.shape
    part_rows = n_rep * rows
    group_rows = n_node * rows
    assert group_rows == row_blocks * tile and part_rows % tile == 0 and tile % rows == 0
    assert width % LANES == 0 and n_node % (width // LANES) == 0
    assert n_node % 2 == 0 and tile // rows % 2 == 0 and width // LANES % 2 == 0
    node_half = n_node // 2
    w_rows = width // n_rep
    w_type = BF16 if w_rows % 16 == 0 else F32
    hbm = pl.BlockSpec(memory_space=pl.ANY)
    dma = pltpu.SemaphoreType.DMA
    node_out, weight_grad, input_grad = pl.pallas_call(
        functools.partial(kernel, n_node, n_rep, float(part_rows * n_node) ** -0.5),
        out_shape=(
            jax.ShapeDtypeStruct((rows, width), BF16),
            jax.ShapeDtypeStruct((w_rows, width), F32),
            jax.ShapeDtypeStruct((rows, width), BF16),
        ),
        in_specs=[pl.BlockSpec(memory_space=pltpu.SMEM)] + [hbm] * 6,
        out_specs=(hbm, hbm, hbm),
        scratch_shapes=[
            pltpu.SMEM((row_blocks, slots), jnp.int32),
            pltpu.VMEM((n_rep, rows, width), BF16),
            pltpu.VMEM((row_blocks, slots, tile, tile), BF16),
            pltpu.VMEM((row_blocks, tile, part_rows), BF16),
            pltpu.VMEM((row_blocks, part_rows, tile), BF16),
            pltpu.VMEM((width, width), BF16),
            pltpu.VMEM((1, width), F32),
            pltpu.VMEM((node_half, rows, width), BF16),
            pltpu.VMEM((2, node_half, rows, width), BF16),
            pltpu.VMEM((node_half, rows, width), BF16),
            pltpu.VMEM((node_half, node_half, rows, width), BF16),
            pltpu.VMEM((2, node_half, rows, width), BF16),
            pltpu.VMEM((width, width // LANES * rows), BF16),
            pltpu.VMEM((2, node_half, rows, width), BF16),
            pltpu.VMEM((node_half, rows, width), BF16),
            pltpu.VMEM((n_rep, w_rows, LANES), w_type),
            pltpu.VMEM((n_rep, w_rows, LANES), w_type),
            pltpu.VMEM((n_node, w_rows, LANES), w_type),
            pltpu.VMEM((w_rows, width), F32),
            pltpu.VMEM((n_rep, rows, width), BF16),
            pltpu.VMEM((n_rep, rows, width), BF16),
            pltpu.VMEM((rows, width), BF16),
            dma((10,)),
            *[dma((n_rep,))] * 6,
            *[dma((node_half,))] * 4,
            *[dma((3,))] * 2,
            *[dma((n_node,))] * 2,
        ],
        compiler_params=pltpu.CompilerParams(
            collective_id=0, has_side_effects=True, vmem_limit_bytes=VMEM_GRANT
        ),
    )(
        tile_count[:, 0],
        *[
            pltpu.with_memory_space_constraint(x, pltpu.HBM)
            for x in (tile_col[:, 0], features, adj_tiles[:, 0], weight, bias.reshape(1, width), out_grad[0])
        ],
    )
    node_out, weight_grad, input_grad = store(node_out, weight_grad, input_grad)
    return node_out[None], weight_grad, input_grad


def solution(mesh):
    return jax.shard_map(
        on_device,
        mesh=mesh,
        in_specs=(
            P(("node", "rep"), None),
            P("rep", "node", None, None, None),
            P("rep", "node", None),
            P("rep", "node"),
            P(),
            P(),
            P("rep", "node", None),
        ),
        out_specs=(P("rep", "node", None), P("rep", None), P(("node", "rep"), None)),
        check_vma=False,
    )
```

```python
import functools

import jax
import jax.numpy as jnp
from jax import lax
from jax.experimental import pallas as pl
from jax.experimental.pallas import tpu as pltpu
from jax.sharding import PartitionSpec as P

LANES = 128
F32 = jnp.float32
BF16 = jnp.bfloat16
MESH = pl.DeviceIdType.MESH
VMEM_GRANT = 40 * 1024 * 1024


def each(start, stop, body):
    if stop - start <= 8:
        for i in range(start, stop):
            body(i)
    else:
        def step(i, carry):
            body(i)
            return carry
        lax.fori_loop(start, stop, step, 0)


def kernel(
    n_node, n_rep, scale,
    counts, cols_in, feat, adj, weight, bias, out_grad,
    node_out, weight_grad, input_grad,
    cols, feat_all, adj_v, dense, dense_t, w_v, bias_v, og_v, sums, sums_in, halves, agg_all, agg_t, pg_all, no_v,
    wg_out, wg_in, wg_fin, wg_v, ig_out, ig_in, ig_v,
    local_sem, f_send, f_recv, w_send, w_recv, i_send, i_recv, o_send, o_recv, s_send, s_recv,
    c_send, c_recv, v_send, v_recv,
):
    s = lax.axis_index("node")
    r = lax.axis_index("rep")
    row_blocks, slots, tile, _ = adj_v.shape
    rows, width = feat.shape
    part_blocks = n_rep * rows // tile
    per_block = tile // rows
    splits = width // LANES
    groups = n_node // splits

    def node_peer(d):
        return lax.rem(s + d, n_node)

    node_half = n_node // 2
    core = lax.rem(s, 2)
    core_pair = s + 1 - 2 * core

    def rep_peer(d):
        return lax.rem(r + d, n_rep)

    def same_core(d):
        return lax.rem(s + 2 * d, n_node)

    def send(axis, peer, src, dst, send_sems, recv_sems, d):
        return pltpu.make_async_remote_copy(
            src_ref=src, dst_ref=dst, send_sem=send_sems.at[d], recv_sem=recv_sems.at[d],
            device_id={axis: peer}, device_id_type=MESH,
        )

    barrier = pltpu.get_barrier_semaphore()
    each(1, n_rep, lambda d: pl.semaphore_signal(barrier, inc=1, device_id={"rep": rep_peer(d)}, device_id_type=MESH))
    each(1, n_node, lambda d: pl.semaphore_signal(barrier, inc=1, device_id={"node": node_peer(d)}, device_id_type=MESH))
    loads = [
        pltpu.make_async_copy(src, dst, local_sem.at[i])
        for i, (src, dst) in enumerate(
            [(feat, feat_all.at[r]), (adj, adj_v), (weight, w_v), (out_grad, og_v.at[lax.div(s, 2)]), (bias, bias_v), (cols_in, cols)]
        )
    ]
    for load in loads:
        load.start()
    loads[0].wait()
    pl.semaphore_wait(barrier, n_rep + n_node - 2)

    def feat_copy(d):
        return send("rep", rep_peer(d), feat_all.at[r], feat_all.at[r], f_send, f_recv, d)
    each(1, n_rep, lambda d: feat_copy(d).start())

    def og_copy(d):
        return send("node", same_core(d), out_grad, og_v.at[lax.div(s, 2)], o_send, o_recv, d)
    each(1, node_half, lambda d: og_copy(d).start())

    loads[1].wait()
    loads[5].wait()
    for b in range(row_blocks):
        def column(c, b=b):
            total = jnp.zeros((tile, tile), F32)
            for k in range(slots):
                live = jnp.logical_and(k < counts[b], cols[b, k] == c)
                total = total + adj_v[b, k].astype(F32) * jnp.where(live, 1.0, 0.0).astype(F32)
            at = pl.ds(pl.multiple_of(c * tile, tile), tile)
            dense[b, :, at] = total.astype(BF16)
            dense_t[b, at, :] = total.T.astype(BF16)
        each(0, part_blocks, column)
    loads[2].wait()
    loads[3].wait()
    loads[4].wait()
    each(1, n_rep, lambda d: feat_copy(d).wait_recv())

    part = feat_all[...].reshape(n_rep * rows, width)
    for b in range(row_blocks):
        value = jnp.dot(dense[b], part, preferred_element_type=F32).astype(BF16)
        value = value.reshape(per_block // 2, 2, rows, width)
        at = slice(b * per_block // 2, (b + 1) * per_block // 2)
        sums[0, at] = value[:, 0]
        sums[1, at] = value[:, 1]

    sum_copy = send("node", core_pair, sums.at[1 - core], sums_in, c_send, c_recv, 0)
    sum_copy.start()
    sum_copy.wait_recv()
    halves[lax.div(s, 2)] = (sums[core].astype(F32) + sums_in[...].astype(F32)).astype(BF16)

    def half_copy(d):
        at = halves.at[lax.div(s, 2)]
        return send("node", same_core(d), at, at, s_send, s_recv, d)
    each(1, node_half, lambda d: half_copy(d).start())
    each(1, node_half, lambda d: og_copy(d).wait_recv())
    each(1, node_half, lambda d: half_copy(d).wait_recv())
    agg = jnp.sum(halves[...].astype(F32), axis=0).astype(BF16)
    agg_all[core] = agg
    agg_copy = send("node", core_pair, agg_all.at[core], agg_all.at[core], c_send, c_recv, 1)
    agg_copy.start()

    preact = jnp.dot(agg.reshape(node_half * rows, width), w_v[...], preferred_element_type=F32) + bias_v[...]
    sigma = lax.logistic(preact)
    cotangent = og_v[...].reshape(node_half * rows, width).astype(F32)
    pre_grad = (cotangent * sigma * (1.0 + preact * (1.0 - sigma))).astype(BF16)
    pg_all[core] = pre_grad.reshape(node_half, rows, width)
    pg_copy = send("node", core_pair, pg_all.at[core], pg_all.at[core], c_send, c_recv, 2)
    pg_copy.start()
    no_v[...] = (preact * sigma).astype(BF16).reshape(node_half, rows, width)
    store_no = pltpu.make_async_copy(no_v.at[lax.div(s, 2)], node_out, local_sem.at[8])
    store_no.start()
    share = splits // 2
    take = pl.ds(lax.div(s, splits) * share, share)
    agg_copy.wait_recv()
    agg_t[...] = agg_all[:, take].reshape(splits * rows, width).T
    pg_copy.wait_recv()

    pg_cols = pg_all[:, take, :, pl.ds(pl.multiple_of(lax.rem(s, splits) * LANES, LANES), LANES)]
    terms = jnp.dot(agg_t[...], pg_cols.reshape(splits * rows, LANES), preferred_element_type=F32)
    wg_out[...] = terms.reshape(wg_out.shape).astype(wg_out.dtype)

    def wg_copy(d):
        return send("rep", rep_peer(d), wg_out.at[rep_peer(d)], wg_in.at[r], w_send, w_recv, d)
    each(1, n_rep, lambda d: wg_copy(d).start())

    up = lax.dot_general(
        pg_all[...].reshape(n_node * rows, width), w_v[...], (((1,), (1,)), ((), ())), preferred_element_type=F32
    ).astype(BF16).reshape(2, node_half, rows, width)
    upstream = jnp.stack([up[i % 2, i // 2] for i in range(n_node)]).reshape(n_node * rows, width)
    grad = jnp.dot(dense_t[0], upstream[:tile], preferred_element_type=F32)
    for b in range(1, row_blocks):
        grad = grad + jnp.dot(dense_t[b], upstream[b * tile:(b + 1) * tile], preferred_element_type=F32)
    ig_out[...] = grad.reshape(ig_out.shape).astype(BF16)

    def ig_copy(d):
        return send("rep", rep_peer(d), ig_out.at[rep_peer(d)], ig_in.at[r], i_send, i_recv, d)
    each(1, n_rep, lambda d: ig_copy(d).start())

    def collect(copy, got, total):
        def add(d, total):
            copy(d).wait_recv()
            return total + got[lax.rem(r + n_rep - d, n_rep)].astype(F32)
        return lax.fori_loop(1, n_rep, add, total, unroll=n_rep <= 8)

    wg_fin[s] = (collect(wg_copy, wg_in, wg_out[r].astype(F32)) * scale).astype(wg_fin.dtype)

    def fin_copy(d):
        return send("node", node_peer(d), wg_fin.at[s], wg_fin.at[s], v_send, v_recv, d)
    each(1, n_node, lambda d: fin_copy(d).start())

    ig_v[...] = collect(ig_copy, ig_in, ig_out[r].astype(F32)).astype(BF16)
    store_ig = pltpu.make_async_copy(ig_v, input_grad, local_sem.at[7])
    store_ig.start()

    each(1, n_node, lambda d: fin_copy(d).wait_recv())
    for c in range(splits):
        total = wg_fin[c].astype(F32)
        for g in range(1, groups):
            total = total + wg_fin[g * splits + c].astype(F32)
        wg_v[:, c * LANES:(c + 1) * LANES] = total
    store_wg = pltpu.make_async_copy(wg_v, weight_grad, local_sem.at[9])
    store_wg.start()

    for copy in (sum_copy, agg_copy, pg_copy):
        copy.wait_send()
    for copy in (feat_copy, wg_copy, ig_copy):
        each(1, n_rep, lambda d: copy(d).wait_send())
    for copy in (og_copy, half_copy):
        each(1, node_half, lambda d: copy(d).wait_send())
    each(1, n_node, lambda d: fin_copy(d).wait_send())
    store_no.wait()
    store_ig.wait()
    store_wg.wait()


def store_kernel(a, b, c, a_out, b_out, c_out, sems):
    copies = [
        pltpu.make_async_copy(src, dst, sems.at[i]) for i, (src, dst) in enumerate([(b, b_out), (a, a_out), (c, c_out)])
    ]
    for copy in copies:
        copy.start()
    for copy in copies:
        copy.wait()


def store(*arrays):
    hbm = pl.BlockSpec(memory_space=pl.ANY)
    return pl.pallas_call(
        store_kernel,
        out_shape=tuple(jax.ShapeDtypeStruct(a.shape, a.dtype) for a in arrays),
        in_specs=[hbm] * 3,
        out_specs=(hbm,) * 3,
        scratch_shapes=[pltpu.SemaphoreType.DMA((3,))],
        compiler_params=pltpu.CompilerParams(vmem_limit_bytes=1024 * 1024),
    )(*arrays)


def on_device(features, adj_tiles, tile_col, tile_count, weight, bias, out_grad):
    n_node = lax.axis_size("node")
    n_rep = lax.axis_size("rep")
    rows, width = features.shape
    row_blocks, _, slots, tile, _ = adj_tiles.shape
    part_rows = n_rep * rows
    group_rows = n_node * rows
    assert group_rows == row_blocks * tile and part_rows % tile == 0 and tile % rows == 0
    assert width % LANES == 0 and n_node % (width // LANES) == 0
    assert n_node % 2 == 0 and tile // rows % 2 == 0 and width // LANES % 2 == 0
    node_half = n_node // 2
    w_rows = width // n_rep
    w_type = BF16 if w_rows % 16 == 0 else F32
    hbm = pl.BlockSpec(memory_space=pl.ANY)
    dma = pltpu.SemaphoreType.DMA
    node_out, weight_grad, input_grad = pl.pallas_call(
        functools.partial(kernel, n_node, n_rep, float(part_rows * n_node) ** -0.5),
        out_shape=(
            jax.ShapeDtypeStruct((rows, width), BF16),
            jax.ShapeDtypeStruct((w_rows, width), F32),
            jax.ShapeDtypeStruct((rows, width), BF16),
        ),
        in_specs=[pl.BlockSpec(memory_space=pltpu.SMEM)] + [hbm] * 6,
        out_specs=(hbm, hbm, hbm),
        scratch_shapes=[
            pltpu.SMEM((row_blocks, slots), jnp.int32),
            pltpu.VMEM((n_rep, rows, width), BF16),
            pltpu.VMEM((row_blocks, slots, tile, tile), BF16),
            pltpu.VMEM((row_blocks, tile, part_rows), BF16),
            pltpu.VMEM((row_blocks, part_rows, tile), BF16),
            pltpu.VMEM((width, width), BF16),
            pltpu.VMEM((1, width), F32),
            pltpu.VMEM((node_half, rows, width), BF16),
            pltpu.VMEM((2, node_half, rows, width), BF16),
            pltpu.VMEM((node_half, rows, width), BF16),
            pltpu.VMEM((node_half, node_half, rows, width), BF16),
            pltpu.VMEM((2, node_half, rows, width), BF16),
            pltpu.VMEM((width, width // LANES * rows), BF16),
            pltpu.VMEM((2, node_half, rows, width), BF16),
            pltpu.VMEM((node_half, rows, width), BF16),
            pltpu.VMEM((n_rep, w_rows, LANES), w_type),
            pltpu.VMEM((n_rep, w_rows, LANES), w_type),
            pltpu.VMEM((n_node, w_rows, LANES), w_type),
            pltpu.VMEM((w_rows, width), F32),
            pltpu.VMEM((n_rep, rows, width), BF16),
            pltpu.VMEM((n_rep, rows, width), BF16),
            pltpu.VMEM((rows, width), BF16),
            dma((10,)),
            *[dma((n_rep,))] * 6,
            *[dma((node_half,))] * 4,
            *[dma((3,))] * 2,
            *[dma((n_node,))] * 2,
        ],
        compiler_params=pltpu.CompilerParams(
            collective_id=0, has_side_effects=True, vmem_limit_bytes=VMEM_GRANT
        ),
    )(
        tile_count[:, 0],
        *[
            pltpu.with_memory_space_constraint(x, pltpu.HBM)
            for x in (tile_col[:, 0], features, adj_tiles[:, 0], weight, bias.reshape(1, width), out_grad[0])
        ],
    )
    node_out, weight_grad, input_grad = store(node_out, weight_grad, input_grad)
    return node_out[None], weight_grad, input_grad


def solution(mesh):
    return jax.shard_map(
        on_device,
        mesh=mesh,
        in_specs=(
            P(("node", "rep"), None),
            P("rep", "node", None, None, None),
            P("rep", "node", None),
            P("rep", "node"),
            P(),
            P(),
            P("rep", "node", None),
        ),
        out_specs=(P("rep", "node", None), P("rep", None), P(("node", "rep"), None)),
        check_vma=False,
    )
```
